32 devices in a mesh: expert: 16 (over z, y, core), dp: 2 (over x).
Axes of the slice: x: 2, y: 2, z: 4, core: 2. Of those that a mesh axis runs over, the one named last changes fastest.
Arguments:
- tokens: bfloat16 [4096, 2048], P(('expert', 'dp')), may hold values from -6 to 6
- d_output: bfloat16 [4096, 2048], P(('expert', 'dp')), may hold values from -6 to 6
- expert_ids: int32 [4096, 8], P(('expert', 'dp')), may hold values from 0 to 15, all different within a row; in each aligned block of 128 rows (0 to 127, 128 to 255, ...) at most 96 rows name the same one
- gate_weights: bfloat16 [4096, 8], P(('expert', 'dp')), may hold values from 0.019897461 to 0.29882812
- pre_acts: bfloat16 [2, 16, 1536, 768], P('dp', 'expert'), may hold values from -6 to 6
- w_gate_up: bfloat16 [16, 2048, 768], P('expert'), may hold values from -0.125 to 0.125
- w_down: bfloat16 [16, 384, 2048], P('expert'), may hold values from -0.3125 to 0.3125
Outputs:
- token_grads: bfloat16 [4096, 2048], P(('expert', 'dp'))
- gate_grads: bfloat16 [4096, 8], P(('expert', 'dp'))
- gate_up_grads: float32 [16, 2048, 768], P('expert', 'dp')
- down_grads: float32 [16, 384, 2048], P('expert', None, 'dp')
The draws below stay inside these ranges and needn't reach their ends.
Inputs may be any that keep to these rules, and one draw needn't show every extreme that they name: `expert_ids`: each token names 8 different experts; among the 128 tokens of one device (aligned blocks) no expert is named by more than 96 tokens, a bound that some block reaches.
All inputs are finite; a program needn't handle non-finite values.
Results may differ from the reference program's by a relative error of at most 0.0057.
Values may be sent and summed in bfloat16 or wider, within the bound.
No kernel may reach another device: no remote copies, remote signals or barrier semaphores. Data moves between devices by JAX's collectives and lax.ppermute only.
A program may use at most 128 MiB of HBM per device.

```python
import math
import jax
import jax.numpy as jnp
import numpy as np
from jax import lax

D = 2048
FF = 384
TOP_K = 8
TOK_DEV = 128
EXPERTS = 16
CAP = 96
REPLICAS = 2
SLOTS = 1536
TOKENS = 4096
N_DP = 2


def level_of(own_key, shape, cuts, low, high):
    loudness, own = 1.0, jax.random.fold_in(own_key, 6)
    for axis_at, shards_of in cuts:
        draws = jnp.exp(jax.random.uniform(jax.random.fold_in(own, axis_at), (shards_of,), jnp.float32, low / len(cuts), high / len(cuts)))
        loudness = loudness * jnp.repeat(draws, shape[axis_at] // shards_of).reshape([-1 if axis == axis_at else 1 for axis in range(len(shape))])
    return loudness


def assign_block(key, own, number, rows, count, top, reach, slope):
    ranking = jax.random.permutation(key, count)
    heavy_load, usual = portions_of(count, rows * top, reach, slope, True), portions_of(count, rows * top, reach, slope, False)
    places = jnp.arange(count)

    def named(lengths, rotation):
        used = int((lengths > 0).sum())
        fixed = max(1, used // 4)
        shifted = fixed + (places - fixed + rotation * (used - fixed)) % max(1, count - fixed)
        return jnp.zeros((count,), jnp.int32).at[ranking[jnp.where(places < fixed, places, shifted)]].set(jnp.asarray(lengths, jnp.int32))

    lengths = jnp.where(number % 4 == 0, named(heavy_load, number // 4), named(usual, number - number // 4 - 1))
    mixed = jax.random.permutation(jax.random.fold_in(own, 3), count)
    source_of, taker = mixed[0:count // 2 * 2:2], mixed[1:count // 2 * 2:2]
    room = jnp.minimum(lengths[source_of] - 1, reach - lengths[taker]) // 2
    room = jnp.where((source_of == ranking[0]) | (taker == ranking[0]) | (lengths[taker] == 0), 0, jnp.maximum(room, 0))
    shifted = jax.random.randint(jax.random.fold_in(own, 4), (count // 2,), 0, 1 << 20) % (room + 1)
    lengths = lengths.at[source_of].add(-shifted).at[taker].add(shifted)
    items = jnp.searchsorted(jnp.cumsum(lengths), jnp.arange(rows * top), side="right").astype(jnp.int32)
    listing = items.reshape(top, rows).T
    listing = listing[jax.random.permutation(jax.random.fold_in(own, 1), rows)]
    rotation = jax.random.randint(jax.random.fold_in(own, 2), (rows, 1), 0, top)
    return jnp.take_along_axis(listing, (jnp.arange(top)[None, :] + rotation) % top, axis=1)


def portions_of(amount, total, reach, lean, full):
    loads = [(1 << 20) // math.isqrt(standing ** lean) + 1 for standing in range(1, amount + 1)]
    largest = reach if full else min(reach, max(-(-total // amount), total * loads[0] // sum(loads)))
    least = 1 if total - largest >= amount - 1 else 0
    given, surplus = [largest] + [least] * (amount - 1), total - largest - least * (amount - 1)
    while surplus > 0:
        free = [i for i in range(1, amount) if given[i] < largest] or [i for i in range(1, amount) if given[i] < reach]
        mass, left = sum([loads[i] for i in free]), surplus
        for i in free:
            addition = min(reach - given[i], max(1, left * loads[i] // mass), surplus)
            given[i] = given[i] + addition
            surplus = surplus - addition
    return np.array(given)


def bell_draw(rng, extent, scale, limit, cuts=(), kind=jnp.bfloat16):
    entries = scale * jax.random.normal(rng, extent, jnp.float32)
    if cuts:
        entries = entries * level_of(rng, extent, cuts, -0.22, 0.18)
    return jnp.clip(entries, -limit, limit).astype(kind)


def setup_inputs(seed: int = 0) -> dict:
    streams_of = jax.random.split(jax.random.key(seed), 8)
    tokens = bell_draw(streams_of[0], (TOKENS, D), 1.0, 6.0, ((0, 32),))
    d_output = bell_draw(streams_of[1], (TOKENS, D), 1.0, 6.0, ((0, 32),))
    expert_ids_keys = jax.random.split(jax.random.fold_in(streams_of[2], 1), TOKENS // TOK_DEV)
    expert_ids_turns = jax.random.permutation(jax.random.fold_in(streams_of[2], 3), TOKENS // TOK_DEV)
    expert_ids = jax.vmap(lambda own, number: assign_block(jax.random.fold_in(streams_of[2], 2), own, number, TOK_DEV, EXPERTS, TOP_K, CAP, 0))(expert_ids_keys, expert_ids_turns).reshape((TOKENS, TOP_K))
    gate_weights = jnp.clip(0.019897461 + 0.27893066 * jax.random.uniform(streams_of[3], (TOKENS, TOP_K), jnp.float32) ** level_of(streams_of[3], (TOKENS, TOP_K), ((0, 32),), -0.2, 0.2), 0.019897461, 0.29882812).astype(jnp.bfloat16)
    pre_acts = bell_draw(streams_of[4], (REPLICAS, EXPERTS, SLOTS, 2 * FF), 1.5, 6.0, ((0, 2), (1, 16)))
    w_gate_up = bell_draw(streams_of[5], (EXPERTS, D, 2 * FF), D ** -0.5, 0.125, ((0, 16),))
    w_down = bell_draw(streams_of[6], (EXPERTS, FF, D), FF ** -0.5, 0.3125, ((0, 16),))
    return {"tokens": tokens, "d_output": d_output, "expert_ids": expert_ids, "gate_weights": gate_weights, "pre_acts": pre_acts, "w_gate_up": w_gate_up, "w_down": w_down}


def contract(left_side, right_side, left_dim, right_dim):
    return lax.dot_general(left_side, right_side, (((left_dim,), (right_dim,)), ((), ())), preferred_element_type=jnp.float32)


def pad_zero(values):
    padding = jnp.zeros((1,) + values.shape[1:], values.dtype)
    return jnp.concatenate([values, padding], axis=0)


def expert_backward(grad_rows, gate_rows, saved_rows, gate_up_weight, down_weight):
    hidden = down_weight.shape[0]
    saved_vals = saved_rows.astype(jnp.float32)
    gate_input = saved_vals[:, :hidden]
    up_input = saved_vals[:, hidden:]
    logistic = jax.nn.sigmoid(gate_input)
    swish_val = gate_input * logistic
    activated = swish_val * up_input
    projected = contract(grad_rows, down_weight, 1, 1)
    gate_grad = jnp.sum(activated * projected, axis=1).astype(jnp.bfloat16)
    weights = gate_rows.astype(jnp.float32)[:, None]
    hidden_grad = weights * projected
    up_grad = hidden_grad * swish_val
    pre_grad = hidden_grad * up_input * logistic * (1.0 + gate_input * (1.0 - logistic))
    both_grad = jnp.concatenate([pre_grad, up_grad], axis=1).astype(jnp.bfloat16)
    scaled = (weights * activated).astype(jnp.bfloat16)
    down_grad = contract(scaled, grad_rows, 0, 0)
    route_grad = contract(both_grad, gate_up_weight, 1, 1).astype(jnp.bfloat16)
    return gate_grad, both_grad, down_grad, route_grad


def block_ranks(block_ids):
    onehot = (block_ids[:, None] == jnp.arange(EXPERTS, dtype=jnp.int32)[None, :]).astype(jnp.int32)
    before = jnp.cumsum(onehot, axis=0) - onehot
    return jnp.sum(before * onehot, axis=1).astype(jnp.int32)


def reference(tokens, d_output, expert_ids, gate_weights, pre_acts, w_gate_up, w_down):
    routes = TOKENS * TOP_K
    blocks = expert_ids.reshape(TOKENS // TOK_DEV, TOK_DEV * TOP_K).astype(jnp.int32)
    route_rank = lax.map(block_ranks, blocks)
    block_index = jnp.arange(TOKENS // TOK_DEV, dtype=jnp.int32)
    source = (block_index // N_DP)[:, None]
    group_index = (block_index % N_DP)[:, None]
    linear = ((group_index * EXPERTS + blocks) * SLOTS + source * CAP + route_rank).reshape(routes).astype(jnp.int32)
    slot_table = jnp.full((N_DP * EXPERTS * SLOTS,), routes, jnp.int32).at[linear].set(jnp.arange(routes, dtype=jnp.int32))
    slot_table = jnp.transpose(slot_table.reshape(N_DP, EXPERTS, SLOTS), (1, 0, 2)).reshape(EXPERTS, N_DP * SLOTS)
    saved_acts = jnp.transpose(pre_acts, (1, 0, 2, 3)).reshape(EXPERTS, N_DP * SLOTS, 2 * FF)
    tokens_pad = pad_zero(tokens)
    grads_pad = pad_zero(d_output)
    gates_pad = pad_zero(gate_weights.reshape(routes))

    def one_expert(carried, inputs):
        row_acc, gate_acc = carried
        pick_rows, saved_rows, gate_up_weight, down_weight = inputs
        token_pick = pick_rows // TOP_K
        input_rows = tokens_pad[token_pick]
        grad_rows = grads_pad[token_pick]
        gate_rows = gates_pad[pick_rows]
        gate_grad, both_grad, down_grad, route_grad = expert_backward(grad_rows, gate_rows, saved_rows, gate_up_weight, down_weight)
        gate_up_grad = contract(input_rows, both_grad, 0, 0)
        row_acc = row_acc.at[token_pick].add(route_grad.astype(jnp.float32))
        gate_acc = gate_acc.at[pick_rows].set(gate_grad.astype(jnp.float32))
        return (row_acc, gate_acc), (gate_up_grad, down_grad)

    initial = (jnp.zeros((TOKENS + 1, D), jnp.float32), jnp.zeros((routes + 1,), jnp.float32))
    (row_acc, gate_acc), (gate_up_grads, down_grads) = lax.scan(one_expert, initial, (slot_table, saved_acts, w_gate_up, w_down))
    token_grads = row_acc[:TOKENS].astype(jnp.bfloat16)
    gate_grads = gate_acc[:routes].reshape(TOKENS, TOP_K).astype(jnp.bfloat16)
    return (token_grads, gate_grads, gate_up_grads, down_grads)
```

```python
import functools

import jax
import jax.numpy as jnp
import numpy as np
from jax import lax
from jax.experimental import pallas as pl
from jax.experimental.pallas import tpu as pltpu
from jax.sharding import PartitionSpec as P

CORES = 2
VMEM = 56 * 1024 * 1024
DEPTH = 2048
ROOMY = 8 * 1024 * 1024


def ring_order(chips):
    return list(range(0, chips, 2)) + list(range(1, chips, 2))[::-1]


def ring_pairs(chips, step):
    order = ring_order(chips)
    return [
        (CORES * chip + core, CORES * order[(at + step) % chips] + core)
        for at, chip in enumerate(order)
        for core in range(CORES)
    ]


def core_pairs(devices):
    return [(i, i ^ 1) for i in range(devices)]


def source_table(devices):
    chips = devices // CORES
    order = ring_order(chips)
    place = {chip: at for at, chip in enumerate(order)}
    table = np.zeros((devices, devices), np.int32)
    for device in range(devices):
        at, core = place[device // CORES], device % CORES
        offsets = [0]
        for far in range(1, chips // 2):
            offsets += [-far, far]
        offsets.append(chips // 2)
        for j, offset in enumerate(offsets):
            chip = order[(at + offset) % chips]
            table[device, 2 * j] = CORES * chip + core
            table[device, 2 * j + 1] = CORES * chip + 1 - core
    return table


def gather_ring(block):
    devices = lax.axis_size("expert")
    chips = devices // CORES
    up, down, across = ring_pairs(chips, 1), ring_pairs(chips, -1), core_pairs(devices)
    half = block.shape[0] // 2
    pairs = [([block], [lax.ppermute(block, "expert", across)])]
    rising = falling = block
    for _ in range(1, chips // 2):
        rising = lax.ppermute(rising, "expert", up)
        falling = lax.ppermute(falling, "expert", down)
        pairs.append(([rising], [lax.ppermute(rising, "expert", across)]))
        pairs.append(([falling], [lax.ppermute(falling, "expert", across)]))
    top = lax.ppermute(rising[:half], "expert", up)
    bottom = lax.ppermute(falling[half:], "expert", down)
    pairs.append(
        ([top, bottom], [lax.ppermute(top, "expert", across), lax.ppermute(bottom, "expert", across)])
    )
    return pairs, rising


def dot(left, right, left_dim, right_dim):
    return lax.dot_general(
        left, right, (((left_dim,), (right_dim,)), ((), ())), preferred_element_type=jnp.float32
    )


def route_kernel(n_own, n_sib, sources, *refs):
    grads, refs = refs[: n_own + n_sib], refs[n_own + n_sib :]
    saved_refs, gate_refs, refs = refs[:2], refs[2:4], refs[4:]
    down_ref, up_ref, both_ref, scaled_ref, gate_grad_ref, own_ref, sib_ref = refs
    hidden = down_ref.shape[0]
    tokens = own_ref.shape[0]
    slots = saved_refs[0].shape[1]
    rows = jnp.concatenate([ref[...] for ref in grads], axis=0)
    projected = dot(rows, down_ref[...], 1, 1)
    line = lax.broadcasted_iota(jnp.int32, (tokens, tokens), 0)
    lane = lax.broadcasted_iota(jnp.int32, (tokens, tokens), 1)
    earlier = (line < lane).astype(jnp.bfloat16)
    diagonal = line == lane
    slot = lax.broadcasted_iota(jnp.int32, (slots, tokens), 0).astype(jnp.float32)
    saved, weights = [], []
    for saved_ref, gate_ref in zip(saved_refs, gate_refs):
        gates = gate_ref[0]
        named = gates > 0.0
        counted = jnp.broadcast_to(named.astype(jnp.bfloat16), (16, tokens))
        rank = dot(counted, earlier, 1, 0)[:1]
        rank = jnp.where(named, rank, -1.0)
        pick = (slot == rank).astype(jnp.bfloat16)
        saved.append(dot(pick, saved_ref[0], 0, 0))
        weights.append(jnp.sum(jnp.where(diagonal, gates, 0.0), axis=1, keepdims=True))
    saved = jnp.concatenate(saved, axis=0)
    weights = jnp.concatenate(weights, axis=0)
    gate_in, up_in = saved[:, :hidden], saved[:, hidden:]
    logistic = jax.nn.sigmoid(gate_in)
    swish = gate_in * logistic
    activated = swish * up_in
    gate_grad = jnp.sum(activated * projected, axis=1, keepdims=True)
    for i in range(2):
        column = gate_grad[i * tokens : (i + 1) * tokens]
        gate_grad_ref[i : i + 1] = jnp.sum(jnp.where(diagonal, column, 0.0), axis=0, keepdims=True)
    hidden_grad = weights * projected
    up_grad = hidden_grad * swish
    pre_grad = hidden_grad * up_in * logistic * (1.0 + gate_in * (1.0 - logistic))
    both = jnp.concatenate([pre_grad, up_grad], axis=1).astype(jnp.bfloat16)
    both_ref[...] = both
    scaled_ref[...] = (weights * activated).astype(jnp.bfloat16)
    route = dot(both, up_ref[...], 1, 1).astype(jnp.bfloat16)
    own_ref[...] = route[:tokens]
    sib_ref[...] = route[tokens:]


def route_pair(j, pair, sources, saved, gates, gate_up_weight, down_weight):
    own, sib = pair
    pieces = own + sib
    width = pieces[0].shape[1]
    tokens = sum(piece.shape[0] for piece in own)
    hidden = down_weight.shape[0]
    slots = saved.shape[1]

    def whole(shape):
        return pl.BlockSpec(shape, lambda i, source: (0,) * len(shape))

    def picked(shape, at):
        return pl.BlockSpec((1,) + shape, lambda i, source: (source[at], 0, 0))

    out_shape = [
        ((2 * tokens, 2 * hidden), jnp.bfloat16),
        ((2 * tokens, hidden), jnp.bfloat16),
        ((2, tokens), jnp.float32),
        ((tokens, width), jnp.bfloat16),
        ((tokens, width), jnp.bfloat16),
    ]
    flops = 2 * 2 * tokens * width * hidden * 3
    return pl.pallas_call(
        functools.partial(route_kernel, len(own), len(sib)),
        grid_spec=pltpu.PrefetchScalarGridSpec(
            num_scalar_prefetch=1,
            grid=(1,),
            in_specs=[whole(piece.shape) for piece in pieces]
            + [picked((slots, 2 * hidden), 0), picked((slots, 2 * hidden), 1)]
            + [picked((1, tokens), 0), picked((1, tokens), 1)]
            + [whole(down_weight.shape), whole(gate_up_weight.shape)],
            out_specs=[whole(shape) for shape, _ in out_shape],
        ),
        out_shape=[jax.ShapeDtypeStruct(*out) for out in out_shape],
        compiler_params=pltpu.CompilerParams(vmem_limit_bytes=VMEM),
        cost_estimate=pl.CostEstimate(flops=flops, bytes_accessed=12 << 20, transcendentals=0),
        name="route",
    )(sources[2 * j : 2 * j + 2], *pieces, saved, saved, gates, gates, down_weight, gate_up_weight)


def weight_kernel(n_wide, n_narrow, wide_first, share, *refs):
    wide, narrow, refs = refs[:n_wide], refs[n_wide : n_wide + n_narrow], refs[n_wide + n_narrow :]
    out_ref, left, right = refs
    at = 0
    for ref in wide:
        left[at : at + ref.shape[0]] = ref[...]
        at += ref.shape[0]

    @pl.when(pl.program_id(0) == 0)
    def _():
        at = 0
        for ref in narrow:
            right[at : at + ref.shape[0]] = ref[...]
            at += ref.shape[0]

    first, second = (left, right) if wide_first else (right, left)
    depth = left.shape[0]
    if depth <= DEPTH or depth % DEPTH:
        out_ref[...] = dot(first[...], second[...], 0, 0).astype(out_ref.dtype)
        return

    def step(k, total):
        part = pl.ds(pl.multiple_of(k * DEPTH, DEPTH), DEPTH)
        return total + dot(first[part], second[part], 0, 0)

    total = lax.fori_loop(0, depth // DEPTH, step, jnp.zeros(out_ref.shape, jnp.float32))
    out_ref[...] = total.astype(out_ref.dtype)


def weight_grad(wide, narrow, share, shares, wide_first, dtype):
    width = wide[0].shape[1]
    part = width // shares
    chunk = min(256, part)
    steps = part // chunk
    depth = sum(piece.shape[0] for piece in wide)
    thin = narrow[0].shape[1]
    if wide_first:
        shape, block, place = (part, thin), (chunk, thin), lambda i, share: (i, 0)
    else:
        shape, block, place = (thin, part), (thin, chunk), lambda i, share: (0, i)
    return pl.pallas_call(
        functools.partial(weight_kernel, len(wide), len(narrow), wide_first),
        grid_spec=pltpu.PrefetchScalarGridSpec(
            num_scalar_prefetch=1,
            grid=(steps,),
            in_specs=[
                pl.BlockSpec((piece.shape[0], chunk), lambda i, share: (0, share[0] * steps + i))
                for piece in wide
            ]
            + [pl.BlockSpec(piece.shape, lambda i, share: (0, 0)) for piece in narrow],
            out_specs=pl.BlockSpec(block, place),
            scratch_shapes=[
                pltpu.VMEM((depth, chunk), wide[0].dtype),
                pltpu.VMEM((depth, thin), narrow[0].dtype),
            ],
        ),
        out_shape=jax.ShapeDtypeStruct(shape, dtype),
        compiler_params=pltpu.CompilerParams(vmem_limit_bytes=VMEM),
        cost_estimate=pl.CostEstimate(
            flops=2 * depth * part * thin, bytes_accessed=depth * (part + thin) * 2, transcendentals=0
        ),
        name="weight_grad",
    )(share, *wide, *narrow)


def shared_weight_grad(wide, narrow, wide_first):
    shares, me = lax.axis_size("dp"), lax.axis_index("dp")
    arrived = []
    for far in range(1, shares):
        theirs = ((me + far) % shares).astype(jnp.int32).reshape(1)
        sent = weight_grad(wide, narrow, theirs, shares, wide_first, jnp.bfloat16)
        arrived.append(lax.ppermute(sent, "dp", [(i, (i + far) % shares) for i in range(shares)]))
    total = weight_grad(wide, narrow, me.astype(jnp.int32).reshape(1), shares, wide_first, jnp.float32)
    return total, arrived


def flat(pairs):
    return [piece for own, sib in pairs for piece in own + sib]


def on_device(tokens, d_output, expert_ids, gate_weights, pre_acts, w_gate_up, w_down):
    devices = lax.axis_size("expert")
    chips = devices // CORES
    up, down, across = ring_pairs(chips, 1), ring_pairs(chips, -1), core_pairs(devices)
    me = lax.axis_index("expert")
    rows = tokens.shape[0]
    half = rows // 2
    table = source_table(devices)
    sources = lax.dynamic_index_in_dim(jnp.asarray(table), me, 0, keepdims=False)
    numbered = lax.dynamic_index_in_dim(jnp.asarray(np.argsort(table, axis=1).astype(np.int32)), me, 0, keepdims=False)

    names = jnp.arange(devices, dtype=jnp.int32)[:, None, None] == expert_ids[None]
    send_gates = jnp.sum(jnp.where(names, gate_weights[None].astype(jnp.float32), 0.0), axis=2)
    gates = lax.all_to_all(
        send_gates.astype(jnp.bfloat16), "expert", split_axis=0, concat_axis=0, tiled=True
    )
    gates = gates.astype(jnp.float32).reshape(devices, 1, rows)
    saved = pre_acts[0, 0].reshape(devices, pre_acts.shape[2] // devices, pre_acts.shape[3])

    grad_pairs, last = gather_ring(d_output)

    roomy = devices * rows * tokens.shape[1] <= ROOMY
    records, shared = [], []
    for j, pair in enumerate(grad_pairs):
        if shared and not roomy:
            sources, _ = lax.optimization_barrier((sources, shared[-1]))
        records.append(route_pair(j, pair, sources, saved, gates, w_gate_up[0], w_down[0]))
        shared.append([records[-1][3], lax.ppermute(records[-1][4], "expert", across)])
        if not roomy:
            shared[-1] = [sum(part.astype(jnp.float32) for part in shared[-1]).astype(jnp.bfloat16)]
    both = [record[0] for record in records]
    scaled = [record[1] for record in records]

    gate_grads = jnp.concatenate([record[2] for record in records], axis=0).astype(jnp.bfloat16)
    home_gates = lax.all_to_all(gate_grads[numbered], "expert", split_axis=0, concat_axis=0, tiled=True)
    gate_out = jnp.sum(jnp.where(names, home_gates.astype(jnp.float32)[:, :, None], 0.0), axis=0)
    gate_out = gate_out.astype(jnp.bfloat16)

    down_total, down_arrived = shared_weight_grad(flat(grad_pairs), scaled, False)

    ahead = (last,) if roomy else (last, down_total, down_arrived)
    tokens = lax.optimization_barrier((tokens,) + ahead)[0]
    token_pairs, last = gather_ring(tokens)

    def added(j, arrived, cut=None):
        total = sum(part.astype(jnp.float32) for part in shared[j])
        if cut is not None:
            total = total[cut]
        for value in arrived:
            total = total + value.astype(jnp.float32)
        return total.astype(jnp.bfloat16)

    rising = added(len(shared) - 1, [], slice(0, half))
    falling = added(len(shared) - 1, [], slice(half, rows))
    rising, falling, _ = lax.optimization_barrier((rising, falling, last))
    rising = jnp.pad(lax.ppermute(rising, "expert", up), ((0, rows - half), (0, 0)))
    falling = jnp.pad(lax.ppermute(falling, "expert", down), ((half, 0), (0, 0)))
    for far in range(chips // 2 - 1, 0, -1):
        rising = lax.ppermute(added(2 * far, [rising]), "expert", up)
        falling = lax.ppermute(added(2 * far - 1, [falling]), "expert", down)
    token_grads = added(0, [rising, falling])

    up_total, up_arrived = shared_weight_grad(flat(token_pairs), both, True)
    for value in up_arrived:
        up_total = up_total + value.astype(jnp.float32)
    for value in down_arrived:
        down_total = down_total + value.astype(jnp.float32)
    return token_grads, gate_out, up_total[None], down_total[None]


def solution(mesh):
    placed = (
        P(("expert", "dp"), None),
        P(("expert", "dp"), None),
        P(("expert", "dp"), None),
        P(("expert", "dp"), None),
        P("dp", "expert", None, None),
        P("expert", None, None),
        P("expert", None, None),
    )
    return jax.shard_map(
        on_device,
        mesh=mesh,
        in_specs=placed,
        out_specs=(
            P(("expert", "dp"), None),
            P(("expert", "dp"), None),
            P("expert", "dp", None),
            P("expert", None, "dp"),
        ),
        check_vma=False,
    )
```

```python
import functools

import jax
import jax.numpy as jnp
import numpy as np
from jax import lax
from jax.experimental import pallas as pl
from jax.experimental.pallas import tpu as pltpu
from jax.sharding import PartitionSpec as P

CORES = 2
VMEM = 24 * 1024 * 1024
DEPTH = 2048
ROUTE_CHUNKS = 4
ROOMY = 8 * 1024 * 1024


def ring_order(chips):
    return list(range(0, chips, 2)) + list(range(1, chips, 2))[::-1]


def ring_pairs(chips, step):
    order = ring_order(chips)
    return [
        (CORES * chip + core, CORES * order[(at + step) % chips] + core)
        for at, chip in enumerate(order)
        for core in range(CORES)
    ]


def core_pairs(devices):
    return [(i, i ^ 1) for i in range(devices)]


def source_table(devices):
    chips = devices // CORES
    order = ring_order(chips)
    place = {chip: at for at, chip in enumerate(order)}
    table = np.zeros((devices, devices), np.int32)
    for device in range(devices):
        at, core = place[device // CORES], device % CORES
        offsets = [0]
        for far in range(1, chips // 2):
            offsets += [-far, far]
        offsets.append(chips // 2)
        for j, offset in enumerate(offsets):
            chip = order[(at + offset) % chips]
            table[device, 2 * j] = CORES * chip + core
            table[device, 2 * j + 1] = CORES * chip + 1 - core
    return table


def dot(left, right, left_dim, right_dim):
    return lax.dot_general(
        left, right, (((left_dim,), (right_dim,)), ((), ())), preferred_element_type=jnp.float32
    )


def route_kernel(counts, sources, *refs):
    blocks = len(counts)
    grads, refs = refs[: sum(counts)], refs[sum(counts) :]
    saved_ref, gate_ref, down_ref, up_ref, both_out, scaled_out, gate_out, refs = *refs[:7], refs[7:]
    outs, (both_ref, scaled_ref, gate_grad_ref, route_ref, sems) = refs[:blocks], refs[blocks:]
    hidden = down_ref.shape[0]
    tokens, width = outs[0].shape
    slots = saved_ref.shape[1]
    rows = jnp.concatenate([ref[...] for ref in grads], axis=0)
    projected = dot(rows, down_ref[...], 1, 1)
    line = lax.broadcasted_iota(jnp.int32, (tokens, tokens), 0)
    lane = lax.broadcasted_iota(jnp.int32, (tokens, tokens), 1)
    earlier = (line < lane).astype(jnp.bfloat16)
    diagonal = line == lane
    slot = lax.broadcasted_iota(jnp.int32, (slots, tokens), 0).astype(jnp.float32)
    saved, weights = [], []
    for i in range(blocks):
        gates = gate_ref[sources[i]]
        named = gates > 0.0
        counted = jnp.broadcast_to(named.astype(jnp.bfloat16), (16, tokens))
        rank = dot(counted, earlier, 1, 0)[:1]
        rank = jnp.where(named, rank, -1.0)
        pick = (slot == rank).astype(jnp.bfloat16)
        saved.append(dot(pick, saved_ref[sources[i]], 0, 0))
        weights.append(jnp.sum(jnp.where(diagonal, gates, 0.0), axis=1, keepdims=True))
    saved = jnp.concatenate(saved, axis=0)
    weights = jnp.concatenate(weights, axis=0)
    gate_in, up_in = saved[:, :hidden], saved[:, hidden:]
    logistic = jax.nn.sigmoid(gate_in)
    swish = gate_in * logistic
    activated = swish * up_in
    gate_grad = jnp.sum(activated * projected, axis=1, keepdims=True)
    for i in range(blocks):
        column = gate_grad[i * tokens : (i + 1) * tokens]
        gate_grad_ref[i : i + 1] = jnp.sum(jnp.where(diagonal, column, 0.0), axis=0, keepdims=True)
    hidden_grad = weights * projected
    up_grad = hidden_grad * swish
    pre_grad = hidden_grad * up_in * logistic * (1.0 + gate_in * (1.0 - logistic))
    both = jnp.concatenate([pre_grad, up_grad], axis=1).astype(jnp.bfloat16)
    both_ref[...] = both
    scaled_ref[...] = (weights * activated).astype(jnp.bfloat16)
    copies = [
        pltpu.make_async_copy(both_ref, both_out, sems.at[0]),
        pltpu.make_async_copy(scaled_ref, scaled_out, sems.at[1]),
        pltpu.make_async_copy(gate_grad_ref, gate_out, sems.at[2]),
    ]
    for copy in copies:
        copy.start()
    chunk = width // ROUTE_CHUNKS
    for part in range(ROUTE_CHUNKS):
        columns = slice(part * chunk, (part + 1) * chunk)
        route_ref[:, columns] = dot(both, up_ref[columns], 1, 1).astype(jnp.bfloat16)
        for i, out in enumerate(outs):
            copies.append(
                pltpu.make_async_copy(
                    route_ref.at[i * tokens : (i + 1) * tokens, columns],
                    out.at[:, columns],
                    sems.at[3 + part * blocks + i],
                )
            )
            copies[-1].start()
    for copy in copies:
        copy.wait()


def in_vmem(count):
    return [pl.BlockSpec(memory_space=pltpu.VMEM)] * count


def in_hbm(count):
    return [pl.BlockSpec(memory_space=pltpu.HBM)] * count


def route_blocks(blocks, sources, saved, gates, gate_up_weight, down_weight):
    pieces = [piece for block in blocks for piece in block]
    width = pieces[0].shape[1]
    tokens = sum(piece.shape[0] for piece in blocks[0])
    hidden = down_weight.shape[0]
    count = len(blocks)
    shapes = [
        ((count * tokens, 2 * hidden), jnp.bfloat16),
        ((count * tokens, hidden), jnp.bfloat16),
        ((count, tokens), jnp.float32),
    ]
    outs = shapes + [((tokens, width), jnp.bfloat16)] * count
    scratch = shapes + [((count * tokens, width), jnp.bfloat16)]
    return pl.pallas_call(
        functools.partial(route_kernel, [len(block) for block in blocks]),
        in_specs=[pl.BlockSpec(memory_space=pltpu.SMEM)] + in_vmem(len(pieces) + 4),
        out_specs=in_hbm(len(outs)),
        out_shape=[pltpu.HBM(*out) for out in outs],
        scratch_shapes=[pltpu.VMEM(*shape) for shape in scratch]
        + [pltpu.SemaphoreType.DMA((3 + ROUTE_CHUNKS * count,))],
        compiler_params=pltpu.CompilerParams(vmem_limit_bytes=VMEM),
        cost_estimate=pl.CostEstimate(
            flops=6 * count * tokens * width * hidden, bytes_accessed=16 << 20, transcendentals=0
        ),
        name="route",
    )(sources, *pieces, saved, gates, down_weight, gate_up_weight)


def weight_kernel(n_wide, n_narrow, wide_first, share, *refs):
    wide, narrow, refs = refs[:n_wide], refs[n_wide : n_wide + n_narrow], refs[n_wide + n_narrow :]
    out_ref, left, right = refs
    at = 0
    for ref in wide:
        left[at : at + ref.shape[0]] = ref[...]
        at += ref.shape[0]

    @pl.when(pl.program_id(0) == 0)
    def _():
        at = 0
        for ref in narrow:
            right[at : at + ref.shape[0]] = ref[...]
            at += ref.shape[0]

    first, second = (left, right) if wide_first else (right, left)
    depth = left.shape[0]
    if depth <= DEPTH or depth % DEPTH:
        out_ref[...] = dot(first[...], second[...], 0, 0).astype(out_ref.dtype)
        return

    def step(k, total):
        part = pl.ds(pl.multiple_of(k * DEPTH, DEPTH), DEPTH)
        return total + dot(first[part], second[part], 0, 0)

    total = lax.fori_loop(0, depth // DEPTH, step, jnp.zeros(out_ref.shape, jnp.float32))
    out_ref[...] = total.astype(out_ref.dtype)


def weight_grad(wide, narrow, share, shares, wide_first, dtype):
    wide, narrow = [[pltpu.with_memory_space_constraint(x, pltpu.HBM) for x in group] for group in (wide, narrow)]
    width = wide[0].shape[1]
    part = width // shares
    chunk = min(512, part)
    steps = part // chunk
    depth = sum(piece.shape[0] for piece in wide)
    thin = narrow[0].shape[1]
    if wide_first:
        shape, block, place = (part, thin), (chunk, thin), lambda i, share: (i, 0)
    else:
        shape, block, place = (thin, part), (thin, chunk), lambda i, share: (0, i)
    return pl.pallas_call(
        functools.partial(weight_kernel, len(wide), len(narrow), wide_first),
        grid_spec=pltpu.PrefetchScalarGridSpec(
            num_scalar_prefetch=1,
            grid=(steps,),
            in_specs=[
                pl.BlockSpec((piece.shape[0], chunk), lambda i, share: (0, share[0] * steps + i))
                for piece in wide
            ]
            + [pl.BlockSpec(piece.shape, lambda i, share: (0, 0)) for piece in narrow],
            out_specs=pl.BlockSpec(block, place),
            scratch_shapes=[
                pltpu.VMEM((depth, chunk), wide[0].dtype),
                pltpu.VMEM((depth, thin), narrow[0].dtype),
            ],
        ),
        out_shape=pltpu.HBM(shape, dtype),
        compiler_params=pltpu.CompilerParams(vmem_limit_bytes=2 * VMEM),
        cost_estimate=pl.CostEstimate(
            flops=2 * depth * part * thin, bytes_accessed=4 * depth * (part + thin) * 2, transcendentals=0
        ),
        name="weight_grad",
    )(share, *wide, *narrow)


def thirds(part):
    units = part // 128
    sizes = [128 * (units // 3 + (i < units % 3)) for i in range(3)]
    return [size for size in sizes if size]


class Ring:
    def __init__(self, block, devices):
        chips = devices // CORES
        self.far = chips // 2
        self.paths = ring_pairs(chips, 1), ring_pairs(chips, -1)
        self.across = core_pairs(devices)
        self.heads = block, block
        self.fresh = [[block]]
        self.own, self.sib = [], []
        self.sent = 0

    def send(self):
        self.sent += 1
        rising, falling = self.heads
        half = rising.shape[0] // 2
        if self.sent == self.far:
            rising, falling = rising[:half], falling[half:]
        rising = lax.ppermute(rising, "expert", self.paths[0])
        falling = lax.ppermute(falling, "expert", self.paths[1])
        self.heads = rising, falling
        return [[rising, falling]] if self.sent == self.far else [[rising], [falling]]

    def share(self):
        for pieces in self.fresh:
            self.own.append(pieces)
            self.sib.append([lax.ppermute(piece, "expert", self.across) for piece in pieces])
        self.fresh = []

    def state(self):
        return self.heads, self.fresh, self.own, self.sib

    def restore(self, state):
        self.heads, self.fresh, self.own, self.sib = state

    def pieces(self):
        return [piece for own, sib in zip(self.own, self.sib) for piece in own + sib]


class Sum:
    def __init__(self, devices, rows):
        chips = devices // CORES
        self.far = chips // 2
        self.paths = ring_pairs(chips, 1), ring_pairs(chips, -1)
        self.half = rows // 2
        self.parts = {}
        self.heads = None
        self.sent = 0

    def total(self, j, arrived=(), cut=slice(None)):
        total = sum(part[cut].astype(jnp.float32) for part in self.parts[j])
        for value in arrived:
            total = total + value.astype(jnp.float32)
        return total.astype(jnp.bfloat16)

    def send(self):
        self.sent += 1
        if self.sent == 1:
            rising = self.total(2 * self.far - 1, (), slice(0, self.half))
            falling = self.total(2 * self.far - 1, (), slice(self.half, None))
        else:
            rising, falling = self.heads
            if self.sent == 2:
                rising = jnp.pad(rising, ((0, self.half), (0, 0)))
                falling = jnp.pad(falling, ((self.half, 0), (0, 0)))
            left = self.far + 1 - self.sent
            rising = self.total(2 * left, [rising])
            falling = self.total(2 * left - 1, [falling])
        rising, falling = fence(rising, falling)
        rising = lax.ppermute(rising, "expert", self.paths[0])
        falling = lax.ppermute(falling, "expert", self.paths[1])
        self.heads = rising, falling


class Swap:
    def __init__(self, values):
        self.shares = len(values) + 1
        self.sizes = thirds(values[0].shape[0])
        self.starts = [sum(self.sizes[:i]) for i in range(len(self.sizes))]
        self.parts = [[value[at : at + size] for value in values] for at, size in zip(self.starts, self.sizes)]
        self.come = []

    def send(self):
        if len(self.come) < len(self.parts):
            parts = self.parts[len(self.come)]
            if self.come:
                parts = fence(parts, self.come[-1])[0]
            self.come.append(
                [
                    lax.ppermute(part, "dp", [(i, (i + k) % self.shares) for i in range(self.shares)])
                    for k, part in enumerate(parts, 1)
                ]
            )

    def add_to(self, total):
        while len(self.come) < len(self.parts):
            self.send()
        for k in range(self.shares - 1):
            arrived = jnp.concatenate([parts[k] for parts in self.come], axis=0)
            total = total + arrived.astype(jnp.float32)
        return total


def fence(*values):
    return lax.optimization_barrier(values)


def on_device(tokens, d_output, expert_ids, gate_weights, pre_acts, w_gate_up, w_down):
    devices = lax.axis_size("expert")
    chips = devices // CORES
    far = chips // 2
    across = core_pairs(devices)
    me = lax.axis_index("expert")
    rows = tokens.shape[0]
    roomy = devices * rows * tokens.shape[1] <= ROOMY
    table = source_table(devices)
    sources = lax.dynamic_index_in_dim(jnp.asarray(table), me, 0, keepdims=False)
    numbered = lax.dynamic_index_in_dim(jnp.asarray(np.argsort(table, axis=1).astype(np.int32)), me, 0, keepdims=False)
    names = jnp.arange(devices, dtype=jnp.int32)[:, None, None] == expert_ids[None]
    saved = pre_acts[0, 0].reshape(devices, pre_acts.shape[2] // devices, pre_acts.shape[3])

    grads, inputs, home = Ring(d_output, devices), Ring(tokens, devices), Sum(devices, rows)
    waiting = {}

    def trade():
        for j in list(waiting):
            own, sib = waiting.pop(j)
            home.parts[j] = [own, lax.ppermute(sib, "expert", across)]
            if not roomy:
                home.parts[j] = [home.total(j)]

    def by(ring, *values):
        ring.heads = fence(ring.heads, values)[0]

    send_gates = jnp.sum(jnp.where(names, gate_weights[None].astype(jnp.float32), 0.0), axis=2)
    gates = lax.all_to_all(send_gates.astype(jnp.bfloat16), "expert", split_axis=0, concat_axis=0, tiled=True)
    gates = gates.astype(jnp.float32).reshape(devices, 1, rows)
    shares, share = lax.axis_size("dp"), lax.axis_index("dp")

    def weight_part(ring, kind, far_share, dtype):
        whose = ((share + far_share) % shares).astype(jnp.int32).reshape(1)
        return weight_grad(ring.pieces(), [record[kind] for record in records], whose, shares, kind == 0, dtype)

    def partners(ring, kind):
        return [weight_part(ring, kind, k, jnp.bfloat16) for k in range(1, shares)]

    records = []

    def work(job):
        if not job:
            return
        blocks = [block for j in job for block in (grads.own[j], grads.sib[j])]
        first = 2 * job[0]
        record = route_blocks(blocks, sources[first : first + len(blocks)], saved, gates, w_gate_up[0], w_down[0])
        records.append(record[:3])
        for i, j in enumerate(job):
            waiting[j] = record[3 + 2 * i : 5 + 2 * i]

    pairs = list(range(chips))
    if roomy and far > 3:
        jobs = [pairs[:1]] + [pairs[2 * k - 1 : 2 * k + 1] for k in range(1, far - 2)]
        jobs += [pairs[2 * far - 5 : 2 * far - 4], pairs[2 * far - 4 : -1], pairs[-1:]]
    else:
        jobs = [pairs[:1]] + [pairs[2 * k - 1 : 2 * k + 1] for k in range(1, far)] + [pairs[-1:]]
    done = 0

    for step in range(1, far + 1):
        if step == 2:
            by(grads, gates)
        if step > 2:
            by(grads, records, home.parts if step == far else ())
        grads.share()
        grads.fresh = grads.send()
        if step > 1:
            if step < far - 1:
                trade()
            work(jobs[done])
            if step == far - 1:
                trade()
            done += 1
    down_swap = None
    if not roomy:
        while done < len(jobs):
            grads.share()
            trade()
            work(jobs[done])
            done += 1
        trade()
        down_swap = Swap(partners(grads, 1))
        down = weight_part(grads, 1, 0, jnp.float32)
        by(inputs, down, down_swap.parts)
        inputs.fresh = [[inputs.heads[0]]]
    for step in range(1, far + 1):
        if roomy:
            by(inputs, grads.heads, records)
        if step == far:
            by(inputs, down_swap.come)
        inputs.share()
        if roomy:
            grads.share()
        inputs.fresh = inputs.send()
        trade()
        if done < len(jobs):
            work(jobs[done])
            done += 1
        elif down_swap is None:
            down_swap = Swap(partners(grads, 1))
            down_swap.send()
    down_swap.send()
    inputs.share()
    gate_grads = jnp.concatenate([record[2] for record in records], axis=0).astype(jnp.bfloat16)
    home_gates = lax.all_to_all(gate_grads[numbered], "expert", split_axis=0, concat_axis=0, tiled=True)
    home.parts = fence(home.parts, inputs.heads, inputs.sib[-1], down_swap.come)[0]
    up_swap = None
    for step in range(1, far + 1):
        if step == 2:
            by(home, up_swap.parts, down_swap.come)
        if step > 2:
            by(home, up_swap.come[: step - 2])
        home.send()
        if step == 1:
            down_swap.send()
            up_swap = Swap(partners(inputs, 0))
        up_swap.send()
    if roomy:
        down = weight_part(grads, 1, 0, jnp.float32)
    down = down_swap.add_to(down)
    up = up_swap.add_to(weight_part(inputs, 0, 0, jnp.float32))
    gate_out = jnp.sum(jnp.where(names, home_gates.astype(jnp.float32)[:, :, None], 0.0), axis=0)
    gate_out = gate_out.astype(jnp.bfloat16)
    token_grads = home.total(0, home.heads)
    return token_grads, gate_out, up[None], down[None]


def solution(mesh):
    placed = (
        P(("expert", "dp"), None),
        P(("expert", "dp"), None),
        P(("expert", "dp"), None),
        P(("expert", "dp"), None),
        P("dp", "expert", None, None),
        P("expert", None, None),
        P("expert", None, None),
    )
    return jax.shard_map(
        on_device,
        mesh=mesh,
        in_specs=placed,
        out_specs=(
            P(("expert", "dp"), None),
            P(("expert", "dp"), None),
            P("expert", "dp", None),
            P("expert", None, "dp"),
        ),
        check_vma=False,
    )
```

```python
import functools

import jax
import jax.numpy as jnp
import numpy as np
from jax import lax
from jax.experimental import pallas as pl
from jax.experimental.pallas import tpu as pltpu
from jax.sharding import PartitionSpec as P

CORES = 2
VMEM = 24 * 1024 * 1024
DEPTH = 512
ROUTE_CHUNKS = 4
LANES = 128
ROOMY = 8 * 1024 * 1024


def ring_order(chips):
    return list(range(0, chips, 2)) + list(range(1, chips, 2))[::-1]


def ring_pairs(chips, step):
    order = ring_order(chips)
    return [
        (CORES * chip + core, CORES * order[(at + step) % chips] + core)
        for at, chip in enumerate(order)
        for core in range(CORES)
    ]


def core_pairs(devices):
    return [(i, i ^ 1) for i in range(devices)]


def source_table(devices):
    chips = devices // CORES
    order = ring_order(chips)
    place = {chip: at for at, chip in enumerate(order)}
    table = np.zeros((devices, devices), np.int32)
    for device in range(devices):
        at, core = place[device // CORES], device % CORES
        offsets = [0]
        for far in range(1, chips // 2):
            offsets += [-far, far]
        offsets.append(chips // 2)
        for j, offset in enumerate(offsets):
            chip = order[(at + offset) % chips]
            table[device, 2 * j] = CORES * chip + core
            table[device, 2 * j + 1] = CORES * chip + 1 - core
    return table


def dot(left, right, left_dim, right_dim):
    return lax.dot_general(
        left, right, (((left_dim,), (right_dim,)), ((), ())), preferred_element_type=jnp.float32
    )


def route_kernel(counts, sources, *refs):
    blocks = len(counts)
    grads, refs = refs[: sum(counts)], refs[sum(counts) :]
    saved_ref, gate_ref, down_ref, up_ref, both_out, scaled_out, refs = *refs[:6], refs[6:]
    outs, (both_ref, scaled_ref, route_ref, sems) = refs[:blocks], refs[blocks:]
    hidden = down_ref.shape[0]
    tokens = outs[0].shape[0]
    width = up_ref.shape[0]
    slots = saved_ref.shape[1]
    rows = jnp.concatenate([ref[...] for ref in grads], axis=0)
    projected = dot(rows, down_ref[...], 1, 1)
    line = lax.broadcasted_iota(jnp.int32, (tokens, tokens), 0)
    lane = lax.broadcasted_iota(jnp.int32, (tokens, tokens), 1)
    earlier = (line < lane).astype(jnp.bfloat16)
    diagonal = line == lane
    slot = lax.broadcasted_iota(jnp.int32, (slots, tokens), 0).astype(jnp.float32)
    saved, weights = [], []
    for i in range(blocks):
        gates = gate_ref[sources[i]]
        named = gates > 0.0
        counted = jnp.broadcast_to(named.astype(jnp.bfloat16), (16, tokens))
        rank = dot(counted, earlier, 1, 0)[:1]
        rank = jnp.where(named, rank, -1.0)
        pick = (slot == rank).astype(jnp.bfloat16)
        saved.append(dot(pick, saved_ref[sources[i]], 0, 0))
        weights.append(jnp.sum(jnp.where(diagonal, gates, 0.0), axis=1, keepdims=True))
    saved = jnp.concatenate(saved, axis=0)
    weights = jnp.concatenate(weights, axis=0)
    gate_in, up_in = saved[:, :hidden], saved[:, hidden:]
    logistic = jax.nn.sigmoid(gate_in)
    swish = gate_in * logistic
    activated = swish * up_in
    gate_grad = jnp.sum(activated * projected, axis=1, keepdims=True)
    extra = route_ref.shape[1] - width
    at_expert = lax.broadcasted_iota(jnp.int32, (blocks * tokens, extra), 1) == sources[blocks]
    route_ref[:, width:] = jnp.where(at_expert, gate_grad, 0.0).astype(jnp.bfloat16)
    hidden_grad = weights * projected
    up_grad = hidden_grad * swish
    pre_grad = hidden_grad * up_in * logistic * (1.0 + gate_in * (1.0 - logistic))
    both = jnp.concatenate([pre_grad, up_grad], axis=1).astype(jnp.bfloat16)
    both_ref[...] = both
    scaled_ref[...] = (weights * activated).astype(jnp.bfloat16)
    copies = [
        pltpu.make_async_copy(both_ref, both_out, sems.at[0]),
        pltpu.make_async_copy(scaled_ref, scaled_out, sems.at[1]),
    ]
    for copy in copies:
        copy.start()
    chunk = width // ROUTE_CHUNKS
    for part in range(ROUTE_CHUNKS):
        columns = slice(part * chunk, (part + 1) * chunk)
        route_ref[:, columns] = dot(both, up_ref[columns], 1, 1).astype(jnp.bfloat16)
        if part == ROUTE_CHUNKS - 1:
            columns = slice(part * chunk, width + extra)
        for i, out in enumerate(outs):
            copies.append(
                pltpu.make_async_copy(
                    route_ref.at[i * tokens : (i + 1) * tokens, columns],
                    out.at[:, columns],
                    sems.at[2 + part * blocks + i],
                )
            )
            copies[-1].start()
    for copy in copies:
        copy.wait()


def in_vmem(count):
    return [pl.BlockSpec(memory_space=pltpu.VMEM)] * count


def in_hbm(count):
    return [pl.BlockSpec(memory_space=pltpu.HBM)] * count


def route_blocks(blocks, sources, saved, gates, gate_up_weight, down_weight):
    pieces = [piece for block in blocks for piece in block]
    width = pieces[0].shape[1]
    tokens = sum(piece.shape[0] for piece in blocks[0])
    hidden = down_weight.shape[0]
    count = len(blocks)
    shapes = [
        ((count * tokens, 2 * hidden), jnp.bfloat16),
        ((count * tokens, hidden), jnp.bfloat16),
    ]
    wider = width + LANES * pl.cdiv(saved.shape[0], LANES)
    outs = shapes + [((tokens, wider), jnp.bfloat16)] * count
    scratch = shapes + [((count * tokens, wider), jnp.bfloat16)]
    return pl.pallas_call(
        functools.partial(route_kernel, [len(block) for block in blocks]),
        in_specs=[pl.BlockSpec(memory_space=pltpu.SMEM)] + in_vmem(len(pieces) + 4),
        out_specs=in_hbm(len(outs)),
        out_shape=[pltpu.HBM(*out) for out in outs],
        scratch_shapes=[pltpu.VMEM(*shape) for shape in scratch]
        + [pltpu.SemaphoreType.DMA((2 + ROUTE_CHUNKS * count,))],
        compiler_params=pltpu.CompilerParams(vmem_limit_bytes=VMEM),
        cost_estimate=pl.CostEstimate(
            flops=6 * count * tokens * width * hidden, bytes_accessed=16 << 20, transcendentals=0
        ),
        name="route",
    )(sources, *pieces, saved, gates, down_weight, gate_up_weight)


def thirds(part):
    units = part // 128
    sizes = [128 * (units // 3 + (i < units % 3)) for i in range(3)]
    return [size for size in sizes if size]


def first_rows(part):
    return [32, part - 32]


def weight_kernel(n_wide, n_narrow, wide_first, share, *refs):
    wide, narrow, refs = refs[:n_wide], refs[n_wide : n_wide + n_narrow], refs[n_wide + n_narrow :]
    outs, (left, right, total, stage, sems) = refs[:-5], refs[-5:]
    depth, part = left.shape
    columns = pl.ds(pl.multiple_of(share[0] * part, 128), part)
    copies = []
    for sources, target, cut in ((wide, left, columns), (narrow, right, slice(None))):
        at = 0
        for ref in sources:
            rows = slice(at, at + ref.shape[0])
            copies.append((at, pltpu.make_async_copy(ref.at[:, cut], target.at[rows], sems.at[len(copies)])))
            at += ref.shape[0]
    copies.sort(key=lambda entry: entry[0])
    for _, copy in copies:
        copy.start()
    first, second = (left, right) if wide_first else (right, left)
    sent = []
    for at in range(0, depth, DEPTH):
        end = min(at + DEPTH, depth)
        while copies and copies[0][0] < end:
            copies.pop(0)[1].wait()
        if end < depth:
            product = dot(first[at:end], second[at:end], 0, 0)
            total[...] = product if at == 0 else total[...] + product
            continue
        start = 0
        for out in outs:
            rows = slice(start, start + out.shape[0])
            product = dot(first[at:end, rows], second[at:end], 0, 0)
            stage[rows] = (product if at == 0 else total[rows] + product).astype(stage.dtype)
            sent.append(pltpu.make_async_copy(stage.at[rows], out, sems.at[n_wide + n_narrow + len(sent)]))
            sent[-1].start()
            start += out.shape[0]
    for copy in sent:
        copy.wait()


def weight_grad(wide, narrow, share, shares, wide_first, dtype, cuts):
    wide, narrow = [[pltpu.with_memory_space_constraint(x, pltpu.HBM) for x in group] for group in (wide, narrow)]
    part = wide[0].shape[1] // shares
    depth = sum(piece.shape[0] for piece in wide)
    thin = narrow[0].shape[1]
    shape = (part, thin) if wide_first else (thin, part)
    sizes = cuts(shape[0]) if cuts else shape[:1]
    return pl.pallas_call(
        functools.partial(weight_kernel, len(wide), len(narrow), wide_first),
        in_specs=[pl.BlockSpec(memory_space=pltpu.SMEM)] + in_hbm(len(wide) + len(narrow)),
        out_specs=in_hbm(len(sizes)),
        out_shape=[pltpu.HBM((size, shape[1]), dtype) for size in sizes],
        scratch_shapes=[
            pltpu.VMEM((depth, part), wide[0].dtype),
            pltpu.VMEM((depth, thin), narrow[0].dtype),
            pltpu.VMEM(shape, jnp.float32),
            pltpu.VMEM(shape, dtype),
            pltpu.SemaphoreType.DMA((len(wide) + len(narrow) + len(sizes),)),
        ],
        compiler_params=pltpu.CompilerParams(vmem_limit_bytes=2 * VMEM),
        cost_estimate=pl.CostEstimate(
            flops=2 * depth * part * thin, bytes_accessed=4 * depth * (part + thin) * 2, transcendentals=0
        ),
        name="weight_grad",
    )(share, *wide, *narrow)


class Ring:
    def __init__(self, block, devices):
        chips = devices // CORES
        self.far = chips // 2
        self.paths = ring_pairs(chips, 1), ring_pairs(chips, -1)
        self.across = core_pairs(devices)
        self.heads = block, block
        self.fresh = [[block]]
        self.own, self.sib = [], []
        self.sent = 0

    def send(self, home=None):
        self.sent += 1
        rising, falling = self.heads
        half = rising.shape[0] // 2
        if self.sent == self.far:
            rising, falling = rising[:half], falling[half:]
        if home is not None:
            sums = home.sums()
            rising, falling = [jnp.concatenate(both, axis=1) for both in ((rising, sums[0]), (falling, sums[1]))]
        rising = lax.ppermute(rising, "expert", self.paths[0])
        falling = lax.ppermute(falling, "expert", self.paths[1])
        if home is not None:
            home.heads = rising, falling
        self.heads = rising, falling
        return [[rising, falling]] if self.sent == self.far else [[rising], [falling]]

    def share(self):
        for pieces in self.fresh:
            self.own.append(pieces)
            self.sib.append([lax.ppermute(piece, "expert", self.across) for piece in pieces])
        self.fresh = []

    def state(self):
        return self.heads, self.fresh, self.own, self.sib

    def restore(self, state):
        self.heads, self.fresh, self.own, self.sib = state

    def pieces(self):
        return [piece for own, sib in zip(self.own, self.sib) for piece in own + sib]


class Sum:
    def __init__(self, devices, rows):
        chips = devices // CORES
        self.far = chips // 2
        self.paths = ring_pairs(chips, 1), ring_pairs(chips, -1)
        self.half = rows // 2
        self.parts = {}
        self.heads = None
        self.sent = 0

    def total(self, j, arrived=(), cut=slice(None)):
        total = sum(part[cut].astype(jnp.float32) for part in self.parts[j])
        for value in arrived:
            total = total + value.astype(jnp.float32)
        return total.astype(jnp.bfloat16)

    def sums(self):
        self.sent += 1
        if self.sent == 1:
            rising = self.total(2 * self.far - 1, (), slice(0, self.half))
            falling = self.total(2 * self.far - 1, (), slice(self.half, None))
        else:
            rising, falling = self.heads
            if self.sent == 2:
                rising, falling = [head[:, head.shape[1] - self.parts[0][0].shape[1] :] for head in (rising, falling)]
                rising = jnp.pad(rising, ((0, self.half), (0, 0)))
                falling = jnp.pad(falling, ((self.half, 0), (0, 0)))
            left = self.far + 1 - self.sent
            rising = self.total(2 * left, [rising])
            falling = self.total(2 * left - 1, [falling])
        return fence(rising, falling)

    def send(self):
        rising, falling = self.sums()
        rising = lax.ppermute(rising, "expert", self.paths[0])
        falling = lax.ppermute(falling, "expert", self.paths[1])
        self.heads = rising, falling


class Swap:
    def __init__(self, values):
        self.shares = len(values) + 1
        self.parts = list(zip(*values))
        self.come = []

    def send(self):
        if len(self.come) < len(self.parts):
            parts = self.parts[len(self.come)]
            if self.come:
                parts = fence(parts, self.come[-1])[0]
            self.come.append(
                [
                    lax.ppermute(part, "dp", [(i, (i + k) % self.shares) for i in range(self.shares)])
                    for k, part in enumerate(parts, 1)
                ]
            )

    def add_to(self, total):
        while len(self.come) < len(self.parts):
            self.send()
        for k in range(self.shares - 1):
            arrived = jnp.concatenate([parts[k] for parts in self.come], axis=0)
            total = total + arrived.astype(jnp.float32)
        return total


def fence(*values):
    return lax.optimization_barrier(values)


def on_device(tokens, d_output, expert_ids, gate_weights, pre_acts, w_gate_up, w_down):
    devices = lax.axis_size("expert")
    chips = devices // CORES
    far = chips // 2
    across = core_pairs(devices)
    me = lax.axis_index("expert")
    rows = tokens.shape[0]
    roomy = devices * rows * tokens.shape[1] <= ROOMY
    table = source_table(devices)
    sources = lax.dynamic_index_in_dim(jnp.asarray(table), me, 0, keepdims=False)
    names = jnp.arange(devices, dtype=jnp.int32)[:, None, None] == expert_ids[None]
    saved = pre_acts[0, 0].reshape(devices, pre_acts.shape[2] // devices, pre_acts.shape[3])

    grads, inputs, home = Ring(d_output, devices), Ring(tokens, devices), Sum(devices, rows)
    waiting = {}

    def trade():
        for j in list(waiting):
            own, sib = waiting.pop(j)
            home.parts[j] = [own, lax.ppermute(sib, "expert", across)]
            if not roomy:
                home.parts[j] = [home.total(j)]

    def by(ring, *values):
        ring.heads = fence(ring.heads, values)[0]

    send_gates = jnp.sum(jnp.where(names, gate_weights[None].astype(jnp.float32), 0.0), axis=2)
    gates = lax.all_to_all(send_gates.astype(jnp.bfloat16), "expert", split_axis=0, concat_axis=0, tiled=True)
    gates = gates.astype(jnp.float32).reshape(devices, 1, rows)
    shares, share = lax.axis_size("dp"), lax.axis_index("dp")

    def weight_part(ring, kind, far_share=0):
        whose = ((share + far_share) % shares).astype(jnp.int32).reshape(1)
        own = far_share == 0
        parts = weight_grad(
            ring.pieces(),
            [record[kind] for record in records],
            whose,
            shares,
            kind == 0,
            jnp.float32 if own else jnp.bfloat16,
            None if own else (thirds if kind == 0 else first_rows),
        )
        return parts[0] if own else parts

    def partners(ring, kind):
        return Swap([weight_part(ring, kind, k) for k in range(1, shares)])

    records = []

    def work(job):
        if not job:
            return
        blocks = [block for j in job for block in (grads.own[j], grads.sib[j])]
        first = 2 * job[0]
        record = route_blocks(blocks, jnp.append(sources[first : first + len(blocks)], me.astype(jnp.int32)), saved, gates, w_gate_up[0], w_down[0])
        records.append(record[:2])
        for i, j in enumerate(job):
            waiting[j] = record[2 + 2 * i : 4 + 2 * i]

    pairs = list(range(chips))
    if roomy and far > 3:
        jobs = [pairs[:1]] + [pairs[2 * k - 1 : 2 * k + 1] for k in range(1, far - 2)]
        jobs += [pairs[2 * far - 5 : 2 * far - 4], pairs[2 * far - 4 : -1], pairs[-1:]]
    else:
        jobs = [pairs[:1]] + [pairs[2 * k - 1 : 2 * k + 1] for k in range(1, far)] + [pairs[-1:]]
    done = 0

    for step in range(1, far + 1):
        if step == 2:
            by(grads, gates)
        if step > 2:
            by(grads, records[: step - 2])
        grads.share()
        grads.fresh = grads.send()
        if step > 1:
            trade()
            work(jobs[done])
            done += 1
    down_swap = down = None
    if not roomy:
        while done < len(jobs):
            grads.share()
            trade()
            work(jobs[done])
            done += 1
        trade()
        down_swap = partners(grads, 1)
        down = weight_part(grads, 1)
        inputs.heads, down, down_swap.parts = fence(inputs.heads, down, down_swap.parts)
        inputs.fresh = [[inputs.heads[0]]]
    for step in range(1, far + 1):
        if roomy:
            by(inputs, grads.heads, records)
        if step == far:
            inputs.heads, home.parts = fence(inputs.heads, home.parts)
        inputs.share()
        if roomy:
            grads.share()
        inputs.fresh = inputs.send(home if step == far else None)
        trade()
        if step == far:
            down_swap.send()
            if roomy:
                down = weight_part(grads, 1)
        elif done < len(jobs):
            work(jobs[done])
            done += 1
        elif down_swap is None:
            down_swap = partners(grads, 1)
            down_swap.send()
    inputs.share()
    up_swap = None
    for step in range(2, far + 1):
        if step == 2:
            by(home, inputs.heads, down_swap.come, down)
        elif step == 3:
            by(home, up_swap.parts)
        elif step == 4:
            by(home, up_swap.come[:1], up)
        home.send()
        if step == 2:
            down_swap.send()
            up_swap = partners(inputs, 0)
        up_swap.send()
        if step == min(3, far):
            up = weight_part(inputs, 0)
    down = down_swap.add_to(down)
    up = up_swap.add_to(up)
    total = home.total(0, home.heads)
    token_grads, gate_grads = total[:, : tokens.shape[1]], total[:, tokens.shape[1] :][:, :devices]
    gate_out = jnp.sum(jnp.where(names, gate_grads.astype(jnp.float32).T[:, :, None], 0.0), axis=0)
    gate_out = gate_out.astype(jnp.bfloat16)
    return token_grads, gate_out, up[None], down[None]


def solution(mesh):
    placed = (
        P(("expert", "dp"), None),
        P(("expert", "dp"), None),
        P(("expert", "dp"), None),
        P(("expert", "dp"), None),
        P("dp", "expert", None, None),
        P("expert", None, None),
        P("expert", None, None),
    )
    return jax.shard_map(
        on_device,
        mesh=mesh,
        in_specs=placed,
        out_specs=(
            P(("expert", "dp"), None),
            P(("expert", "dp"), None),
            P("expert", "dp", None),
            P("expert", None, "dp"),
        ),
        check_vma=False,
    )
```

```python
import functools

import jax
import jax.numpy as jnp
import numpy as np
from jax import lax
from jax.experimental import pallas as pl
from jax.experimental.pallas import tpu as pltpu
from jax.sharding import PartitionSpec as P

CORES = 2
VMEM = 24 * 1024 * 1024
DEPTH = 512
ROUTE_CHUNKS = 4
LANES = 128
ROOMY = 8 * 1024 * 1024


def ring_order(chips):
    return list(range(0, chips, 2)) + list(range(1, chips, 2))[::-1]


def ring_pairs(chips, step):
    order = ring_order(chips)
    return [
        (CORES * chip + core, CORES * order[(at + step) % chips] + core)
        for at, chip in enumerate(order)
        for core in range(CORES)
    ]


def core_pairs(devices):
    return [(i, i ^ 1) for i in range(devices)]


def source_table(devices):
    chips = devices // CORES
    order = ring_order(chips)
    place = {chip: at for at, chip in enumerate(order)}
    table = np.zeros((devices, devices), np.int32)
    for device in range(devices):
        at, core = place[device // CORES], device % CORES
        offsets = [0]
        for far in range(1, chips // 2):
            offsets += [-far, far]
        offsets.append(chips // 2)
        for j, offset in enumerate(offsets):
            chip = order[(at + offset) % chips]
            table[device, 2 * j] = CORES * chip + core
            table[device, 2 * j + 1] = CORES * chip + 1 - core
    return table


def dot(left, right, left_dim, right_dim):
    return lax.dot_general(
        left, right, (((left_dim,), (right_dim,)), ((), ())), preferred_element_type=jnp.float32
    )


def route_kernel(counts, sources, *refs):
    blocks = len(counts)
    grads, refs = refs[: sum(counts)], refs[sum(counts) :]
    saved_ref, gate_ref, down_ref, up_ref, both_out, scaled_out, refs = *refs[:6], refs[6:]
    outs, (both_ref, scaled_ref, route_ref, sems) = refs[:blocks], refs[blocks:]
    hidden = down_ref.shape[0]
    tokens = outs[0].shape[0]
    width = up_ref.shape[0]
    slots = saved_ref.shape[1]
    rows = jnp.concatenate([ref[...] for ref in grads], axis=0)
    projected = dot(rows, down_ref[...], 1, 1)
    line = lax.broadcasted_iota(jnp.int32, (tokens, tokens), 0)
    lane = lax.broadcasted_iota(jnp.int32, (tokens, tokens), 1)
    earlier = (line < lane).astype(jnp.bfloat16)
    diagonal = line == lane
    slot = lax.broadcasted_iota(jnp.int32, (slots, tokens), 0).astype(jnp.float32)
    saved, weights = [], []
    for i in range(blocks):
        gates = gate_ref[sources[i]]
        named = gates > 0.0
        counted = jnp.broadcast_to(named.astype(jnp.bfloat16), (16, tokens))
        rank = dot(counted, earlier, 1, 0)[:1]
        rank = jnp.where(named, rank, -1.0)
        pick = (slot == rank).astype(jnp.bfloat16)
        saved.append(dot(pick, saved_ref[sources[i]], 0, 0))
        weights.append(jnp.sum(jnp.where(diagonal, gates, 0.0), axis=1, keepdims=True))
    saved = jnp.concatenate(saved, axis=0)
    weights = jnp.concatenate(weights, axis=0)
    gate_in, up_in = saved[:, :hidden], saved[:, hidden:]
    logistic = jax.nn.sigmoid(gate_in)
    swish = gate_in * logistic
    activated = swish * up_in
    gate_grad = jnp.sum(activated * projected, axis=1, keepdims=True)
    extra = route_ref.shape[1] - width
    at_expert = lax.broadcasted_iota(jnp.int32, (blocks * tokens, extra), 1) == sources[blocks]
    route_ref[:, width:] = jnp.where(at_expert, gate_grad, 0.0).astype(jnp.bfloat16)
    hidden_grad = weights * projected
    up_grad = hidden_grad * swish
    pre_grad = hidden_grad * up_in * logistic * (1.0 + gate_in * (1.0 - logistic))
    both = jnp.concatenate([pre_grad, up_grad], axis=1).astype(jnp.bfloat16)
    both_ref[...] = both
    scaled_ref[...] = (weights * activated).astype(jnp.bfloat16)
    copies = [
        pltpu.make_async_copy(both_ref, both_out, sems.at[0]),
        pltpu.make_async_copy(scaled_ref, scaled_out, sems.at[1]),
    ]
    for copy in copies:
        copy.start()
    chunk = width // ROUTE_CHUNKS
    for part in range(ROUTE_CHUNKS):
        columns = slice(part * chunk, (part + 1) * chunk)
        route_ref[:, columns] = dot(both, up_ref[columns], 1, 1).astype(jnp.bfloat16)
        if part == ROUTE_CHUNKS - 1:
            columns = slice(part * chunk, width + extra)
        for i, out in enumerate(outs):
            copies.append(
                pltpu.make_async_copy(
                    route_ref.at[i * tokens : (i + 1) * tokens, columns],
                    out.at[:, columns],
                    sems.at[2 + part * blocks + i],
                )
            )
            copies[-1].start()
    for copy in copies:
        copy.wait()


def in_vmem(count):
    return [pl.BlockSpec(memory_space=pltpu.VMEM)] * count


def in_hbm(count):
    return [pl.BlockSpec(memory_space=pltpu.HBM)] * count


def route_blocks(blocks, sources, saved, gates, gate_up_weight, down_weight):
    pieces = [piece for block in blocks for piece in block]
    width = pieces[0].shape[1]
    tokens = sum(piece.shape[0] for piece in blocks[0])
    hidden = down_weight.shape[0]
    count = len(blocks)
    shapes = [
        ((count * tokens, 2 * hidden), jnp.bfloat16),
        ((count * tokens, hidden), jnp.bfloat16),
    ]
    wider = width + LANES * pl.cdiv(saved.shape[0], LANES)
    outs = shapes + [((tokens, wider), jnp.bfloat16)] * count
    scratch = shapes + [((count * tokens, wider), jnp.bfloat16)]
    return pl.pallas_call(
        functools.partial(route_kernel, [len(block) for block in blocks]),
        in_specs=[pl.BlockSpec(memory_space=pltpu.SMEM)] + in_vmem(len(pieces) + 4),
        out_specs=in_hbm(len(outs)),
        out_shape=[pltpu.HBM(*out) for out in outs],
        scratch_shapes=[pltpu.VMEM(*shape) for shape in scratch]
        + [pltpu.SemaphoreType.DMA((2 + ROUTE_CHUNKS * count,))],
        compiler_params=pltpu.CompilerParams(vmem_limit_bytes=VMEM),
        cost_estimate=pl.CostEstimate(
            flops=6 * count * tokens * width * hidden, bytes_accessed=16 << 20, transcendentals=0
        ),
        name="route",
    )(sources, *pieces, saved, gates, down_weight, gate_up_weight)


def cut_rows(part):
    quarter = max(128, part // 512 * 128)
    sizes = [part - 2 * quarter, quarter, quarter]
    return [size for size in sizes if size > 0]


def first_rows(part):
    return [32, part - 32]


def weight_kernel(n_wide, n_narrow, wide_first, share, *refs):
    wide, narrow, refs = refs[:n_wide], refs[n_wide : n_wide + n_narrow], refs[n_wide + n_narrow :]
    outs, (left, right, total, stage, sems) = refs[:-5], refs[-5:]
    depth, part = left.shape
    columns = pl.ds(pl.multiple_of(share[0] * part, 128), part)
    copies = []
    for sources, target, cut in ((wide, left, columns), (narrow, right, slice(None))):
        at = 0
        for ref in sources:
            rows = slice(at, at + ref.shape[0])
            copies.append((at, pltpu.make_async_copy(ref.at[:, cut], target.at[rows], sems.at[len(copies)])))
            at += ref.shape[0]
    copies.sort(key=lambda entry: entry[0])
    for _, copy in copies:
        copy.start()
    first, second = (left, right) if wide_first else (right, left)
    sent = []
    for at in range(0, depth, DEPTH):
        end = min(at + DEPTH, depth)
        while copies and copies[0][0] < end:
            copies.pop(0)[1].wait()
        if end < depth:
            product = dot(first[at:end], second[at:end], 0, 0)
            total[...] = product if at == 0 else total[...] + product
            continue
        start = 0
        if len(outs) == 1:
            product = dot(first[at:end], second[at:end], 0, 0)
            outs[0][...] = (product if at == 0 else total[...] + product).astype(outs[0].dtype)
            break
        for out in outs:
            rows = slice(start, start + out.shape[0])
            product = dot(first[at:end, rows], second[at:end], 0, 0)
            stage[rows] = (product if at == 0 else total[rows] + product).astype(stage.dtype)
            sent.append(pltpu.make_async_copy(stage.at[rows], out, sems.at[n_wide + n_narrow + len(sent)]))
            sent[-1].start()
            start += out.shape[0]
    for copy in sent:
        copy.wait()


def weight_grad(wide, narrow, share, shares, wide_first, dtype, cuts):
    wide, narrow = [[pltpu.with_memory_space_constraint(x, pltpu.HBM) for x in group] for group in (wide, narrow)]
    part = wide[0].shape[1] // shares
    depth = sum(piece.shape[0] for piece in wide)
    thin = narrow[0].shape[1]
    shape = (part, thin) if wide_first else (thin, part)
    sizes = cuts(shape[0]) if cuts else shape[:1]
    return pl.pallas_call(
        functools.partial(weight_kernel, len(wide), len(narrow), wide_first),
        in_specs=[pl.BlockSpec(memory_space=pltpu.SMEM)] + in_hbm(len(wide) + len(narrow)),
        out_specs=in_hbm(len(sizes)) if cuts else in_vmem(1),
        out_shape=[pltpu.HBM((size, shape[1]), dtype) for size in sizes]
        if cuts
        else [jax.ShapeDtypeStruct(shape, dtype)],
        scratch_shapes=[
            pltpu.VMEM((depth, part), wide[0].dtype),
            pltpu.VMEM((depth, thin), narrow[0].dtype),
            pltpu.VMEM(shape, jnp.float32),
            pltpu.VMEM(shape if cuts else (8, 128), dtype),
            pltpu.SemaphoreType.DMA((len(wide) + len(narrow) + len(sizes),)),
        ],
        compiler_params=pltpu.CompilerParams(vmem_limit_bytes=2 * VMEM),
        cost_estimate=pl.CostEstimate(
            flops=2 * depth * part * thin, bytes_accessed=4 * depth * (part + thin) * 2, transcendentals=0
        ),
        name="weight_grad",
    )(share, *wide, *narrow)


def add_kernel(at, total_ref, *refs):
    parts, (out_ref, held, sems) = refs[:-3], refs[-3:]
    rows = pl.ds(at, held.shape[0])
    read = pltpu.make_async_copy(total_ref.at[rows], held, sems.at[0])
    read.start()
    read.wait()
    for part in parts:
        held[...] += part[...].astype(jnp.float32)
    write = pltpu.make_async_copy(held, out_ref.at[rows], sems.at[1])
    write.start()
    write.wait()


def add_rows(total, parts, at):
    size = parts[0].shape[0]
    return pl.pallas_call(
        functools.partial(add_kernel, at),
        in_specs=in_hbm(1) + in_vmem(len(parts)),
        out_specs=pl.BlockSpec(memory_space=pltpu.HBM),
        out_shape=pltpu.HBM(total.shape, total.dtype),
        input_output_aliases={0: 0},
        scratch_shapes=[
            pltpu.VMEM((size, total.shape[1]), total.dtype),
            pltpu.SemaphoreType.DMA((2,)),
        ],
        compiler_params=pltpu.CompilerParams(vmem_limit_bytes=VMEM),
        cost_estimate=pl.CostEstimate(flops=size * total.shape[1], bytes_accessed=8 * size * total.shape[1], transcendentals=0),
        name="add_rows",
    )(total, *parts)


class Ring:
    def __init__(self, block, devices):
        chips = devices // CORES
        self.far = chips // 2
        self.paths = ring_pairs(chips, 1), ring_pairs(chips, -1)
        self.across = core_pairs(devices)
        self.heads = block, block
        self.fresh = [[block]]
        self.own, self.sib = [], []
        self.sent = 0

    def send(self, home=None):
        self.sent += 1
        rising, falling = self.heads
        half = rising.shape[0] // 2
        if self.sent == self.far:
            rising, falling = rising[:half], falling[half:]
        if home is not None:
            sums = home.sums()
            rising, falling = [jnp.concatenate(both, axis=1) for both in ((rising, sums[0]), (falling, sums[1]))]
        rising = lax.ppermute(rising, "expert", self.paths[0])
        falling = lax.ppermute(falling, "expert", self.paths[1])
        if home is not None:
            home.heads = rising, falling
        self.heads = rising, falling
        return [[rising, falling]] if self.sent == self.far else [[rising], [falling]]

    def share(self):
        for pieces in self.fresh:
            self.own.append(pieces)
            self.sib.append([lax.ppermute(piece, "expert", self.across) for piece in pieces])
        self.fresh = []

    def state(self):
        return self.heads, self.fresh, self.own, self.sib

    def restore(self, state):
        self.heads, self.fresh, self.own, self.sib = state

    def pieces(self):
        return [piece for own, sib in zip(self.own, self.sib) for piece in own + sib]


class Sum:
    def __init__(self, devices, rows):
        chips = devices // CORES
        self.far = chips // 2
        self.paths = ring_pairs(chips, 1), ring_pairs(chips, -1)
        self.half = rows // 2
        self.parts = {}
        self.heads = None
        self.sent = 0

    def total(self, j, arrived=(), cut=slice(None)):
        total = sum(part[cut].astype(jnp.float32) for part in self.parts[j])
        for value in arrived:
            total = total + value.astype(jnp.float32)
        return total.astype(jnp.bfloat16)

    def sums(self):
        self.sent += 1
        if self.sent == 1:
            rising = self.total(2 * self.far - 1, (), slice(0, self.half))
            falling = self.total(2 * self.far - 1, (), slice(self.half, None))
        else:
            rising, falling = self.heads
            if self.sent == 2:
                rising, falling = [head[:, head.shape[1] - self.parts[0][0].shape[1] :] for head in (rising, falling)]
                rising = jnp.pad(rising, ((0, self.half), (0, 0)))
                falling = jnp.pad(falling, ((self.half, 0), (0, 0)))
            left = self.far + 1 - self.sent
            rising = self.total(2 * left, [rising])
            falling = self.total(2 * left - 1, [falling])
        return fence(rising, falling)

    def send(self):
        rising, falling = self.sums()
        rising = lax.ppermute(rising, "expert", self.paths[0])
        falling = lax.ppermute(falling, "expert", self.paths[1])
        self.heads = rising, falling


class Swap:
    def __init__(self, values):
        self.shares = len(values) + 1
        self.parts = list(zip(*values))
        self.come = []

    def send(self):
        if len(self.come) < len(self.parts):
            parts = self.parts[len(self.come)]
            if self.come:
                parts = fence(parts, self.come[-1])[0]
            self.come.append(
                [
                    lax.ppermute(part, "dp", [(i, (i + k) % self.shares) for i in range(self.shares)])
                    for k, part in enumerate(parts, 1)
                ]
            )

    def add_to(self, total):
        while len(self.come) < len(self.parts):
            self.send()
        at = 0
        for parts in self.come:
            total = add_rows(total, parts, at)
            at += parts[0].shape[0]
        return total


def fence(*values):
    return lax.optimization_barrier(values)


def on_device(tokens, d_output, expert_ids, gate_weights, pre_acts, w_gate_up, w_down):
    devices = lax.axis_size("expert")
    chips = devices // CORES
    far = chips // 2
    across = core_pairs(devices)
    me = lax.axis_index("expert")
    rows = tokens.shape[0]
    roomy = devices * rows * tokens.shape[1] <= ROOMY
    table = source_table(devices)
    sources = lax.dynamic_index_in_dim(jnp.asarray(table), me, 0, keepdims=False)
    names = jnp.arange(devices, dtype=jnp.int32)[:, None, None] == expert_ids[None]
    saved = pre_acts[0, 0].reshape(devices, pre_acts.shape[2] // devices, pre_acts.shape[3])

    grads, inputs, home = Ring(d_output, devices), Ring(tokens, devices), Sum(devices, rows)
    waiting = {}

    def trade():
        for j in list(waiting):
            own, sib = waiting.pop(j)
            home.parts[j] = [own, lax.ppermute(sib, "expert", across)]
            if not roomy:
                home.parts[j] = [home.total(j)]

    def by(ring, *values):
        ring.heads = fence(ring.heads, values)[0]

    send_gates = jnp.sum(jnp.where(names, gate_weights[None].astype(jnp.float32), 0.0), axis=2)
    gates = lax.all_to_all(send_gates.astype(jnp.bfloat16), "expert", split_axis=0, concat_axis=0, tiled=True)
    gates = gates.astype(jnp.float32).reshape(devices, 1, rows)
    shares, share = lax.axis_size("dp"), lax.axis_index("dp")

    def weight_part(ring, kind, far_share=0):
        whose = ((share + far_share) % shares).astype(jnp.int32).reshape(1)
        own = far_share == 0
        parts = weight_grad(
            ring.pieces(),
            [record[kind] for record in records],
            whose,
            shares,
            kind == 0,
            jnp.float32 if own else jnp.bfloat16,
            None if own else (cut_rows if kind == 0 else first_rows),
        )
        return parts[0] if own else parts

    def partners(ring, kind):
        return Swap([weight_part(ring, kind, k) for k in range(1, shares)])

    records = []

    def work(job):
        if not job:
            return
        blocks = [block for j in job for block in (grads.own[j], grads.sib[j])]
        first = 2 * job[0]
        record = route_blocks(blocks, jnp.append(sources[first : first + len(blocks)], me.astype(jnp.int32)), saved, gates, w_gate_up[0], w_down[0])
        records.append(record[:2])
        for i, j in enumerate(job):
            waiting[j] = record[2 + 2 * i : 4 + 2 * i]

    pairs = list(range(chips))
    if roomy and far > 3:
        jobs = [pairs[:1]] + [pairs[2 * k - 1 : 2 * k + 1] for k in range(1, far - 2)]
        jobs += [pairs[2 * far - 5 : 2 * far - 4], pairs[2 * far - 4 : -1], pairs[-1:]]
    else:
        jobs = [pairs[:1]] + [pairs[2 * k - 1 : 2 * k + 1] for k in range(1, far)] + [pairs[-1:]]
    done = 0

    for step in range(1, far + 1):
        if step == 2:
            by(grads, gates)
        if step > 2:
            by(grads, records[: step - 2])
        grads.share()
        grads.fresh = grads.send()
        if step > 1:
            trade()
            work(jobs[done])
            done += 1
    down_swap = down = None
    if not roomy:
        while done < len(jobs):
            grads.share()
            trade()
            work(jobs[done])
            done += 1
        trade()
        down_swap = partners(grads, 1)
        down = weight_part(grads, 1)
        inputs.heads, down, down_swap.parts = fence(inputs.heads, down, down_swap.parts)
        inputs.fresh = [[inputs.heads[0]]]
    for step in range(1, far + 1):
        if roomy:
            by(inputs, grads.heads, records)
        if step == far:
            inputs.heads, home.parts = fence(inputs.heads, home.parts)
        inputs.share()
        if roomy:
            grads.share()
        inputs.fresh = inputs.send(home if step == far else None)
        trade()
        if step == far:
            down_swap.send()
            if roomy:
                down = weight_part(grads, 1)
        elif done < len(jobs):
            work(jobs[done])
            done += 1
        elif down_swap is None:
            down_swap = partners(grads, 1)
            down_swap.send()
    inputs.share()
    up_swap = None
    for step in range(2, far + 1):
        if step == 2:
            by(home, inputs.heads, down_swap.come)
            home.heads, down = fence(home.heads, down)
        elif step == 3:
            by(home, up_swap.parts)
        elif step == 4:
            by(home, up_swap.come[:1])
            home.heads, up = fence(home.heads, up)
        home.send()
        if step == 2:
            down_swap.send()
            up_swap = partners(inputs, 0)
        up_swap.send()
        if step == min(3, far):
            up = weight_part(inputs, 0)
    down = down_swap.add_to(down)
    up = up_swap.add_to(up)
    total = home.total(0, home.heads)
    token_grads, gate_grads = total[:, : tokens.shape[1]], total[:, tokens.shape[1] :][:, :devices]
    gate_out = jnp.sum(jnp.where(names, gate_grads.astype(jnp.float32).T[:, :, None], 0.0), axis=0)
    gate_out = gate_out.astype(jnp.bfloat16)
    return token_grads, gate_out, up[None], down[None]


def solution(mesh):
    placed = (
        P(("expert", "dp"), None),
        P(("expert", "dp"), None),
        P(("expert", "dp"), None),
        P(("expert", "dp"), None),
        P("dp", "expert", None, None),
        P("expert", None, None),
        P("expert", None, None),
    )
    return jax.shard_map(
        on_device,
        mesh=mesh,
        in_specs=placed,
        out_specs=(
            P(("expert", "dp"), None),
            P(("expert", "dp"), None),
            P("expert", "dp", None),
            P("expert", None, "dp"),
        ),
        check_vma=False,
    )
```
